256 devices in a mesh: scene: 64 (over z_hi, y, x, core), view: 4 (over z_lo).
Axes of the slice: x: 4, y: 4, z: 8 (z_hi: 2, z_lo: 4; z = z_hi * 4 + z_lo), core: 2. Of those that a mesh axis runs over, the one named last changes fastest.
Arguments:
- queries: bfloat16 [64, 4, 512, 1024], P('scene', 'view'), may hold values from -6 to 6
- keys: bfloat16 [64, 4, 512, 1024], P('scene', 'view'), may hold values from -6 to 6
- values: bfloat16 [64, 4, 512, 1024], P('scene', 'view'), may hold values from -6 to 6
- out_grad: bfloat16 [64, 4, 512, 2048], P('scene', 'view'), may hold values from -1.5 to 1.5
- w_out: bfloat16 [1024, 2048], replicated, may hold values from -0.1875 to 0.1875
- bucket_of: int32 [64, 4, 4], P('scene'), may hold values from 0 to 3, as said below
- pair_mask: int32 [64, 4, 4], P('scene'), may hold values from 0 to 1, as said below
Outputs:
- layer_out: bfloat16 [64, 4, 512, 2048], P('scene', 'view')
- grad_queries: bfloat16 [64, 4, 512, 1024], P('scene', 'view')
- grad_keys: bfloat16 [64, 4, 512, 1024], P('scene', 'view')
- grad_values: bfloat16 [64, 4, 512, 1024], P('scene', 'view')
- grad_w_out: bfloat16 [1024, 2048], replicated
The draws below stay inside these ranges and needn't reach their ends.
Inputs may be any that keep to these rules, and one draw needn't show every extreme that they name: `bucket_of`: each view's 4 blocks lie in 4 different buckets; in every scene one bucket holds a block of every view. pair_mask[s, a, a] = 1 for every view a.
All inputs are finite; a program needn't handle non-finite values.
Results may differ from the reference program's by a relative error of at most 0.008.
Values may be sent and summed in bfloat16 or wider, within the bound.
A program may use at most 128 MiB of HBM per device.

```python
import math
import jax
import jax.numpy as jnp
from jax import lax

D = 2048
HEADS = 8
HDIM = 128
BLK = 128
TOK = 512
SCENES = 64
N_VIEW = 4


def draw_queries(key, part):
    full_shape = (SCENES, N_VIEW, TOK, HEADS * HDIM)
    sample = jax.random.truncated_normal(jax.random.fold_in(key, 1), -6.0, 6.0, full_shape, jnp.float32)
    return sample.astype(jnp.bfloat16)


def draw_keys(key, part):
    full_shape = (SCENES, N_VIEW, TOK, HEADS * HDIM)
    sample = jax.random.truncated_normal(jax.random.fold_in(key, 2), -6.0, 6.0, full_shape, jnp.float32)
    return sample.astype(jnp.bfloat16)


def draw_bucket_of(key, part):
    hottest = jax.random.randint(jax.random.fold_in(key, 21), (SCENES, 1, 1), 0, N_VIEW)
    pick_keys = jax.random.split(jax.random.fold_in(key, 22), SCENES * N_VIEW)
    others = jax.vmap(lambda subkey: jax.random.permutation(subkey, N_VIEW - 1))(pick_keys)
    others = others.reshape(SCENES, N_VIEW, N_VIEW - 1)[:, :, :TOK // BLK - 1]
    others = (hottest + 1 + others) % N_VIEW
    listed = jnp.concatenate([jnp.broadcast_to(hottest, (SCENES, N_VIEW, 1)), others], axis=2)
    order_keys = jax.random.split(jax.random.fold_in(key, 23), SCENES * N_VIEW)
    ordering = jax.vmap(lambda subkey: jax.random.permutation(subkey, TOK // BLK))(order_keys)
    ordering = ordering.reshape(SCENES, N_VIEW, TOK // BLK)
    return jnp.take_along_axis(listed, ordering, axis=2).astype(jnp.int32)


def draw_pair_mask(key, part):
    random_bits = jax.random.randint(jax.random.fold_in(key, 31), (SCENES, N_VIEW, N_VIEW), 0, 2)
    diagonal = jnp.arange(N_VIEW)[:, None] == jnp.arange(N_VIEW)[None, :]
    return jnp.where(diagonal[None], 1, random_bits).astype(jnp.int32)


def block_scale(stream_key, shape, pieces, low, top_value):
    factor_of, own = 1.0, jax.random.fold_in(stream_key, 6)
    for dim, blocks in pieces:
        heights = jnp.exp(jax.random.uniform(jax.random.fold_in(own, dim), (blocks,), jnp.float32, low / len(pieces), top_value / len(pieces)))
        factor_of = factor_of * jnp.repeat(heights, shape[dim] // blocks).reshape([-1 if axis == dim else 1 for axis in range(len(shape))])
    return factor_of


def bell_draw(key, shape, scale, reach, cuts=(), kind=jnp.bfloat16):
    values = jax.random.normal(key, shape, jnp.float32) * scale
    if len(cuts) > 0:
        values = block_scale(key, shape, cuts, -0.22, 0.18) * values
    return jnp.clip(values, min=-reach, max=reach).astype(kind)


def setup_inputs(seed: int = 0) -> dict:
    arg_keys = jax.random.split(jax.random.key(seed), 8)
    return {
        "queries": draw_queries(jax.random.fold_in(arg_keys[7], 71), 0),
        "keys": draw_keys(jax.random.fold_in(arg_keys[7], 71), 0),
        "values": bell_draw(arg_keys[2], (SCENES, N_VIEW, TOK, HEADS * HDIM), 1.0, 6.0, ((0, 64), (1, 4))),
        "out_grad": bell_draw(arg_keys[3], (SCENES, N_VIEW, TOK, D), 0.25, 1.5, ((0, 64), (1, 4))),
        "w_out": bell_draw(arg_keys[4], (HEADS * HDIM, D), (HEADS * HDIM) ** -0.5, 0.1875),
        "bucket_of": draw_bucket_of(jax.random.fold_in(arg_keys[7], 71), 0),
        "pair_mask": draw_pair_mask(jax.random.fold_in(arg_keys[7], 71), 0),
    }


NEG_FILL = -1e+30

def bucket_pass(queries_b, keys_b, values_b, grads_b, allowed):
    inv_root = 1.0 / math.sqrt(HDIM)
    query_f = queries_b.astype(jnp.float32)
    key_f = keys_b.astype(jnp.float32)
    value_f = values_b.astype(jnp.float32)
    grad_f = grads_b.astype(jnp.float32)
    scores = jnp.einsum('ihe,jhe->hij', query_f, key_f) * inv_root
    scores = jnp.where(allowed[None], scores, NEG_FILL)
    peak = lax.optimization_barrier(jnp.max(scores, axis=-1, keepdims=True))
    exponent = jnp.exp(scores - peak)
    weights = exponent / lax.optimization_barrier(jnp.sum(exponent, axis=-1, keepdims=True))
    weights_b = lax.optimization_barrier(weights.astype(jnp.bfloat16)).astype(jnp.float32)
    attended = jnp.einsum('hij,jhe->ihe', weights_b, value_f).astype(jnp.bfloat16)
    grad_weights = jnp.einsum('ihe,jhe->hij', grad_f, value_f)
    row_dot = lax.optimization_barrier(jnp.sum(weights * grad_weights, axis=-1, keepdims=True))
    grad_scores = (weights * (grad_weights - row_dot) * inv_root).astype(jnp.bfloat16)
    grad_scores = lax.optimization_barrier(grad_scores).astype(jnp.float32)
    grad_query = jnp.einsum('hij,jhe->ihe', grad_scores, key_f).astype(jnp.bfloat16)
    grad_key = jnp.einsum('hij,ihe->jhe', grad_scores, query_f).astype(jnp.bfloat16)
    grad_value = jnp.einsum('hij,ihe->jhe', weights_b, grad_f).astype(jnp.bfloat16)
    return (attended, grad_query, grad_key, grad_value)

def reference(queries, keys, values, out_grad, w_out, bucket_of, pair_mask):
    width = HEADS * HDIM
    rows_all = N_VIEW * BLK
    nblocks = TOK // BLK
    weight_f = w_out.astype(jnp.float32)

    def scene_pass(carry, inputs):
        queries_s, keys_s, values_s, out_grad_s, bucket_s, pair_s = inputs
        grad_f = out_grad_s.astype(jnp.float32)
        grad_attn = jnp.einsum('vtd,fd->vtf', grad_f, weight_f).astype(jnp.bfloat16)
        stacked = [tensor.astype(jnp.float32).reshape(N_VIEW, nblocks, BLK, width) for tensor in (queries_s, keys_s, values_s, grad_attn)]

        def bucket_step(totals, bucket_id):
            selector = (bucket_s == bucket_id).astype(jnp.float32)
            gathered = [jnp.einsum('vb,vbrf->vrf', selector, tensor).astype(jnp.bfloat16).reshape(rows_all, HEADS, HDIM) for tensor in stacked]
            live_src = lax.optimization_barrier(jnp.sum(selector, axis=1)) > 0
            allowed_blocks = (pair_s > 0) & live_src[None, :]
            allowed = jnp.repeat(jnp.repeat(allowed_blocks, BLK, axis=0), BLK, axis=1)
            results = bucket_pass(gathered[0], gathered[1], gathered[2], gathered[3], allowed)
            updated = tuple((total + jnp.einsum('vb,vrf->vbrf', selector, result.reshape(N_VIEW, BLK, width).astype(jnp.float32)) for total, result in zip(totals, results)))
            return (updated, None)
        zeros_f = jnp.zeros((N_VIEW, nblocks, BLK, width), jnp.float32)
        totals, _ = lax.scan(bucket_step, (zeros_f, zeros_f, zeros_f, zeros_f), jnp.arange(N_VIEW, dtype=jnp.int32))
        finished = [total.reshape(N_VIEW, TOK, width).astype(jnp.bfloat16) for total in totals]
        attended_f = finished[0].astype(jnp.float32)
        layer_out = jnp.einsum('vtf,fd->vtd', attended_f, weight_f).astype(jnp.bfloat16)
        carry = carry + jnp.einsum('vtf,vtd->fd', attended_f, grad_f)
        return (carry, (layer_out, finished[1], finished[2], finished[3]))
    start = jnp.zeros((width, D), jnp.float32)
    grad_total, outputs = lax.scan(scene_pass, start, (queries, keys, values, out_grad, bucket_of, pair_mask))
    layer_out, grad_queries, grad_keys, grad_values = outputs
    return (layer_out, grad_queries, grad_keys, grad_values, grad_total.astype(jnp.bfloat16))
```

```python
import functools
import math

import jax
import jax.numpy as jnp
from jax import lax
from jax.experimental import pallas as pl
from jax.experimental.pallas import tpu as pltpu
from jax.sharding import PartitionSpec as P

HDIM = 128
BLK = 128
NEG_FILL = -1e30
MESH = pl.DeviceIdType.MESH
F32 = jnp.float32
BF16 = jnp.bfloat16
REDUCE = True
TIMING = False
PINNED = True
NT = (((1,), (1,)), ((), ()))
TN = (((0,), (0,)), ((), ()))


def dot(a, b, dims=(((1,), (0,)), ((), ()))):
    return lax.dot_general(a, b, dims, preferred_element_type=F32)


def place(core, y, x, z_hi):
    return ((z_hi * 4 + y) * 4 + x) * 2 + core


def kernel(
    heads,
    views,
    q_hbm, k_hbm, v_hbm, og_hbm, w_hbm, bucket_ref, pair_ref,
    lo_ref, gq_ref, gk_ref, gv_ref, gw_ref,
    qkv_in, og, w, snd, rcv, ga_buf, ga_snd, ga_rcv, mask, wts, gs, gs_t,
    att_snd, att_rcv, att, att_t, g_snd, g_rcv,
    load_sem, big_sem, qs_sem, qr_sem, as_sem, ar_sem, gs_sem, gr_sem, bs_sem, br_sem,
    *reduce_refs,
):
    scene = lax.axis_index("scene")
    me = lax.axis_index("view")
    rows = views * BLK
    inv_root = 1.0 / math.sqrt(HDIM)
    offsets = range(1, views)
    at = [lax.rem(me + o, views) for o in range(views)]
    came = [lax.rem(me + views - o, views) for o in range(views)]

    peers = [(scene, at[o]) for o in offsets]
    if REDUCE:
        part, gsum, r0, r1, r2, zsrc, rz, zg, cs, cr, s1s, s1r, s2s, s2r, zs, zr, ts, tr, g2s, g2r, g1s, g1r, gcs, gcr = reduce_refs
        core = lax.rem(scene, 2)
        x = lax.rem(scene // 2, 4)
        y = lax.rem(scene // 8, 4)
        z_hi = scene // 32
        z = z_hi * 4 + me
        first_x = 1 - core
        i1 = first_x * x + core * y
        i2 = first_x * y + core * x
        other = (place(1 - core, y, x, z_hi), me)
        axis1, axis2, along_z = [], [], []
        for o in range(1, 4):
            x1, y1 = lax.rem(x + o * first_x, 4), lax.rem(y + o * core, 4)
            x2, y2 = lax.rem(x + o * core, 4), lax.rem(y + o * first_x, 4)
            axis1.append((place(core, y1, x1, z_hi), me))
            axis2.append((place(core, y2, x2, z_hi), me))
        for o in range(1, 8):
            zz = lax.rem(z + o, 8)
            along_z.append((place(core, y, x, zz // 4), lax.rem(zz, 4)))
        peers = [other] + axis1 + axis2 + along_z

    barrier = pltpu.get_barrier_semaphore()
    for peer in peers:
        pl.semaphore_signal(barrier, inc=1, device_id=peer, device_id_type=MESH)

    loads = []
    for part_id, cols in enumerate((pl.ds(0, 2 * HDIM), pl.ds(2 * HDIM, (heads - 2) * HDIM))):
        for t, ref in enumerate((q_hbm, k_hbm, v_hbm)):
            copy = pltpu.make_async_copy(
                ref.at[:, :, cols], qkv_in.at[t, :, :, cols], load_sem.at[t, part_id]
            )
            copy.start()
            loads.append(copy)
    w_load = pltpu.make_async_copy(w_hbm, w, big_sem.at[0])
    og_load = pltpu.make_async_copy(og_hbm, og, big_sem.at[1])
    og_load.start()
    w_load.start()

    block_at = []
    for o in range(views):
        found = jnp.int32(0)
        for j in range(views):
            found = jnp.where(bucket_ref[me, j] == at[o], j, found)
        block_at.append(found)
    lane_view = lax.broadcasted_iota(jnp.int32, (1, rows), 1) // BLK
    for a in range(views):
        row = jnp.zeros((1, rows), F32)
        for b in range(views):
            live = jnp.int32(0)
            for j in range(views):
                live = live + jnp.where(bucket_ref[b, j] == me, 1, 0)
            ok = jnp.where((pair_ref[a, b] > 0) & (live > 0), 1.0, 0.0)
            row = row + jnp.where(lane_view == b, ok, 0.0)
        mask[a] = row

    def cols_of(h, n=1):
        return pl.ds(pl.multiple_of(h * HDIM, HDIM), n * HDIM)

    def qkv_copy(h, o, to):
        slot = at[o] if to else came[o]
        return pltpu.make_async_remote_copy(
            src_ref=snd.at[h, :, at[o]],
            dst_ref=rcv.at[h, :, me if to else slot],
            send_sem=qs_sem.at[h, o],
            recv_sem=qr_sem.at[h, o],
            device_id=(scene, at[o]),
            device_id_type=MESH,
        )

    def ga_copy(h, o, to):
        return pltpu.make_async_remote_copy(
            src_ref=ga_snd.at[h, at[o]],
            dst_ref=ga_rcv.at[h, me if to else came[o]],
            send_sem=as_sem.at[h, o],
            recv_sem=ar_sem.at[h, o],
            device_id=(scene, at[o]),
            device_id_type=MESH,
        )

    def att_copy(h, o, to):
        return pltpu.make_async_remote_copy(
            src_ref=att_snd.at[h, at[o]],
            dst_ref=att_rcv.at[h, me if to else came[o]],
            send_sem=bs_sem.at[h, o],
            recv_sem=br_sem.at[h, o],
            device_id=(scene, at[o]),
            device_id_type=MESH,
        )

    def grad_copy(h, o, to):
        return pltpu.make_async_remote_copy(
            src_ref=g_snd.at[h, :, at[o]],
            dst_ref=g_rcv.at[h, :, me if to else came[o]],
            send_sem=gs_sem.at[h, o],
            recv_sem=gr_sem.at[h, o],
            device_id=(scene, at[o]),
            device_id_type=MESH,
        )

    def pick(which, blocks):
        block = blocks[0]
        for j in range(1, views):
            block = lax.select_n(which == j, block, blocks[j])
        return block

    def send_qkv(h, carry):
        for t in range(3):
            blocks = [qkv_in[t, j, :, cols_of(h)] for j in range(views)]
            for o in range(views):
                block = pick(block_at[o], blocks)
                if o == 0:
                    rcv[h, t, me] = block
                else:
                    snd[h, t, at[o]] = block
        for o in offsets:
            qkv_copy(h, o, True).start()
        return carry

    for copy in loads[:3]:
        copy.wait()
    pl.semaphore_wait(barrier, len(peers))
    lax.fori_loop(0, 2, send_qkv, 0)
    for copy in loads[3:]:
        copy.wait()
    lax.fori_loop(2, heads, send_qkv, 0)

    og_load.wait()
    w_load.wait()

    def make_ga(p, carry):
        ga = dot(og[...], w[pl.ds(pl.multiple_of(p * 2 * HDIM, 2 * HDIM), 2 * HDIM), :], NT)
        ga_buf[:, :, cols_of(2 * p, 2)] = ga.astype(BF16).reshape(views, BLK, 2 * HDIM)
        for s in range(2):
            h = 2 * p + s
            for o in range(views):
                block = ga_buf[block_at[o], :, cols_of(h)]
                if o == 0:
                    ga_rcv[h, me] = block
                else:
                    ga_snd[h, at[o]] = block
        return carry

    lax.fori_loop(0, heads // 2, make_ga, 0)

    def forward(h, carry):
        for o in offsets:
            qkv_copy(h, o, False).wait_recv()
        keys = rcv[h, 1].reshape(rows, HDIM)
        values = rcv[h, 2].reshape(rows, HDIM)
        for o in (1, 2, 3, 0):
            a = at[o]
            scores = dot(rcv[h, 0, a], keys, NT) * inv_root
            scores = jnp.where(mask[a] > 0.5, scores, NEG_FILL)
            peak = jnp.max(scores, axis=1, keepdims=True)
            exponent = jnp.exp(scores - peak)
            weights = exponent * (1.0 / jnp.sum(exponent, axis=1, keepdims=True))
            wts[h, a] = weights
            attended = dot(weights.astype(BF16), values).astype(BF16)
            if o == 0:
                att_rcv[h, me] = attended
            else:
                att_snd[h, a] = attended
                att_copy(h, o, True).start()
        return carry

    lax.fori_loop(0, heads, forward, 0)

    def send_ga(h, carry):
        for o in offsets:
            ga_copy(h, o, True).start()
        return carry

    lax.fori_loop(0, heads, send_ga, 0)

    def backward(h, carry):
        for o in offsets:
            ga_copy(h, o, False).wait_recv()
        keys = rcv[h, 1].reshape(rows, HDIM)
        values = rcv[h, 2].reshape(rows, HDIM)
        for a in range(views):
            weights = wts[h, a]
            grad_weights = dot(ga_rcv[h, a], values, NT)
            row_dot = jnp.sum(weights * grad_weights, axis=1, keepdims=True)
            grad_scores = (weights * (grad_weights - row_dot) * inv_root).astype(BF16)
            gs[pl.ds(a * BLK, BLK), :] = grad_scores
            gs_t[pl.ds(a * BLK, BLK), :] = weights.astype(BF16)
            g_snd[h, 0, a] = dot(grad_scores, keys).astype(BF16)
        queries = rcv[h, 0].reshape(rows, HDIM)
        grads = ga_rcv[h].reshape(rows, HDIM)
        grad_keys = dot(queries, gs[...], TN).T
        g_snd[h, 1] = grad_keys.astype(BF16).reshape(views, BLK, HDIM)
        grad_values = dot(grads, gs_t[...], TN).T
        g_snd[h, 2] = grad_values.astype(BF16).reshape(views, BLK, HDIM)
        for o in offsets:
            grad_copy(h, o, True).start()
        g_rcv[h, :, me] = g_snd[h, :, me]
        return carry

    home = [bucket_ref[me, j] for j in range(views)]

    def unpack_att(h, carry):
        for o in offsets:
            att_copy(h, o, False).wait_recv()
        blocks = [att_rcv[h, b] for b in range(views)]
        for j in range(views):
            block = pick(home[j], blocks)
            att[pl.ds(j * BLK, BLK), cols_of(h)] = block
            att_t[cols_of(h), pl.ds(j * BLK, BLK)] = block.T
        return carry

    width = heads * HDIM
    wide = 256

    def make_out(c, carry):
        cols = pl.ds(pl.multiple_of(c * wide, wide), wide)
        lo_ref[:, cols] = dot(att[...], w[:, cols]).astype(BF16)
        return carry

    def make_part(c, carry):
        span = pl.ds(pl.multiple_of(c * wide, wide), wide)
        for d in range(og.shape[1] // 512):
            cols = pl.ds(d * 512, 512)
            term = dot(att_t[span, :], og[:, cols])
            if REDUCE:
                part[span, cols] = term.astype(BF16)
            else:
                gw_ref[span, cols] = term
        return carry

    lax.fori_loop(0, heads, unpack_att, 0)
    lax.fori_loop(0, width // wide, make_part, 0)
    if REDUCE:
        half = width // 2
        core_rows = pl.ds(pl.multiple_of(core * half, half), half)
        other_rows = pl.ds(pl.multiple_of((1 - core) * half, half), half)

        def remote(src, dst, s_sem, r_sem, to):
            return pltpu.make_async_remote_copy(
                src_ref=src, dst_ref=dst, send_sem=s_sem, recv_sem=r_sem,
                device_id=to, device_id_type=MESH,
            )

        c_copy = remote(part.at[other_rows], r0, cs, cr, other)
        c_copy.start()
    lax.fori_loop(0, lo_ref.shape[1] // wide, make_out, 0)

    if not REDUCE:
        lax.fori_loop(0, heads, backward, 0)
    else:
        lax.fori_loop(0, 1, backward, 0)
        c_copy.wait()

        def sum_core(i, carry):
            piece = pl.ds(pl.multiple_of(i * 32, 32), 32)
            mine = pl.ds(pl.multiple_of(core * half + i * 32, 32), 32)
            gsum[piece] = (part[mine].astype(F32) + r0[piece].astype(F32)).astype(BF16)
            return carry

        lax.fori_loop(0, half // 32, sum_core, 0)

        def rows_of(i, n):
            return pl.ds(pl.multiple_of(i * n, n), n)

        rs1 = [
            remote(gsum.at[rows_of(lax.rem(i1 + o, 4), 128)], r1.at[o - 1], s1s.at[o - 1], s1r.at[o - 1], axis1[o - 1])
            for o in range(1, 4)
        ]
        for copy in rs1:
            copy.start()
        lax.fori_loop(1, 2, backward, 0)
        for copy in rs1:
            copy.wait()

        def sum_1(i, carry):
            piece = pl.ds(pl.multiple_of(i * 32, 32), 32)
            total = gsum[pl.ds(pl.multiple_of(i1 * 128 + i * 32, 32), 32)].astype(F32)
            for o in range(3):
                total = total + r1[o, piece].astype(F32)
            r0[piece] = total.astype(BF16)
            return carry

        lax.fori_loop(0, 4, sum_1, 0)
        rs2 = [
            remote(r0.at[rows_of(lax.rem(i2 + o, 4), 32)], r2.at[o - 1], s2s.at[o - 1], s2r.at[o - 1], axis2[o - 1])
            for o in range(1, 4)
        ]
        for copy in rs2:
            copy.start()
        for copy in rs2:
            copy.wait()
        total = r0[rows_of(i2, 32)].astype(F32)
        for o in range(3):
            total = total + r2[o].astype(F32)
        total = total.astype(BF16)
        for p in range(8):
            zsrc[p] = total[:, p * 256:(p + 1) * 256]
        rsz = [
            remote(zsrc.at[lax.rem(z + o, 8)], rz.at[o - 1], zs.at[o - 1], zr.at[o - 1], along_z[o - 1])
            for o in range(1, 8)
        ]
        for copy in rsz:
            copy.start()
        lax.fori_loop(2, 3, backward, 0)
        for copy in rsz:
            copy.wait()
        total = zsrc[z].astype(F32)
        for o in range(7):
            total = total + rz[o].astype(F32)
        zg[z] = total.astype(BF16)
        agz = [
            remote(zg.at[z], zg.at[z], ts.at[o - 1], tr.at[o - 1], along_z[o - 1])
            for o in range(1, 8)
        ]
        for copy in agz:
            copy.start()
        lax.fori_loop(3, 4, backward, 0)
        for o in range(1, 8):
            src = zg.at[lax.rem(z + 8 - o, 8)]
            remote(src, src, ts.at[o - 1], tr.at[o - 1], along_z[o - 1]).wait()
        for p in range(8):
            gw_ref[core, i1, i2, :, pl.ds(p * 256, 256)] = zg[p]
        ag2 = []
        for o in range(1, 4):
            spot = gw_ref.at[core, i1, i2]
            remote(spot, spot, g2s.at[o - 1], g2r.at[o - 1], axis2[o - 1]).start()
        lax.fori_loop(4, 5, backward, 0)
        for o in range(1, 4):
            spot = gw_ref.at[core, i1, lax.rem(i2 + 4 - o, 4)]
            remote(spot, spot, g2s.at[o - 1], g2r.at[o - 1], axis2[o - 1]).wait()
        for o in range(1, 4):
            spot = gw_ref.at[core, i1]
            remote(spot, spot, g1s.at[o - 1], g1r.at[o - 1], axis1[o - 1]).start()
        lax.fori_loop(5, heads, backward, 0)
        for o in range(1, 4):
            spot = gw_ref.at[core, lax.rem(i1 + 4 - o, 4)]
            remote(spot, spot, g1s.at[o - 1], g1r.at[o - 1], axis1[o - 1]).wait()
        spot = gw_ref.at[core]
        remote(spot, spot, gcs, gcr, other).start()

    def finish(h, carry):
        for o in offsets:
            grad_copy(h, o, False).wait_recv()
        for t, ref in enumerate((gq_ref, gk_ref, gv_ref)):
            blocks = [g_rcv[h, t, b] for b in range(views)]
            for j in range(views):
                ref[j, :, cols_of(h)] = pick(home[j], blocks)
        for o in offsets:
            qkv_copy(h, o, True).wait_send()
            ga_copy(h, o, True).wait_send()
            att_copy(h, o, True).wait_send()
            grad_copy(h, o, True).wait_send()
        return carry

    lax.fori_loop(0, heads, finish, 0)
    if REDUCE:
        spot = gw_ref.at[1 - core]
        remote(spot, spot, gcs, gcr, other).wait()


def write_out(*refs):
    count = (len(refs) - 1) // 2
    sems = refs[-1]
    copies = [
        pltpu.make_async_copy(refs[i], refs[count + i], sems.at[i]) for i in range(count)
    ]
    for copy in copies:
        copy.start()
    for copy in copies:
        copy.wait()


def body(queries, keys, values, out_grad, w_out, bucket_of, pair_mask):
    views = lax.axis_size("view")
    tokens, width = queries.shape[2:]
    heads = width // HDIM
    model = out_grad.shape[-1]
    rows = views * BLK
    blocks = (views, BLK, width)
    vmem = pl.BlockSpec(memory_space=pltpu.VMEM)
    smem = pl.BlockSpec(memory_space=pltpu.SMEM)
    hbm = pl.BlockSpec(memory_space=pl.ANY)
    dma = pltpu.SemaphoreType.DMA
    scratch = [
        pltpu.VMEM((3,) + blocks, BF16),
        pltpu.VMEM((tokens, model), BF16),
        pltpu.VMEM((width, model), BF16),
        pltpu.VMEM((heads, 3, views, BLK, HDIM), BF16),
        pltpu.VMEM((heads, 3, views, BLK, HDIM), BF16),
        pltpu.VMEM(blocks, BF16),
        pltpu.VMEM((heads, views, BLK, HDIM), BF16),
        pltpu.VMEM((heads, views, BLK, HDIM), BF16),
        pltpu.VMEM((views, 1, rows), F32),
        pltpu.VMEM((heads, views, BLK, rows), F32),
        pltpu.VMEM((rows, rows), BF16),
        pltpu.VMEM((rows, rows), BF16),
        pltpu.VMEM((heads, views, BLK, HDIM), BF16),
        pltpu.VMEM((heads, views, BLK, HDIM), BF16),
        pltpu.VMEM((tokens, width), BF16),
        pltpu.VMEM((width, tokens), BF16),
        pltpu.VMEM((heads, 3, views, BLK, HDIM), BF16),
        pltpu.VMEM((heads, 3, views, BLK, HDIM), BF16),
        dma((3, 2)),
        dma((2,)),
    ] + [dma((heads, views))] * 8
    if REDUCE:
        scratch += [
            pltpu.VMEM((width, model), BF16),
            pltpu.VMEM((width // 2, model), BF16),
            pltpu.VMEM((width // 2, model), BF16),
            pltpu.VMEM((3, 128, model), BF16),
            pltpu.VMEM((3, 32, model), BF16),
            pltpu.VMEM((8, 32, model // 8), BF16),
            pltpu.VMEM((7, 32, model // 8), BF16),
            pltpu.VMEM((8, 32, model // 8), BF16),
            dma, dma,
            dma((3,)), dma((3,)), dma((3,)), dma((3,)),
            dma((7,)), dma((7,)), dma((7,)), dma((7,)),
            dma((3,)), dma((3,)), dma((3,)), dma((3,)),
            dma, dma,
        ]
        gw_shape = jax.ShapeDtypeStruct((2, 4, 4, 32, model), BF16)
    else:
        gw_shape = jax.ShapeDtypeStruct((width, model), F32)
    grad_shape = jax.ShapeDtypeStruct(blocks, BF16)
    shapes = (
        jax.ShapeDtypeStruct((tokens, model), BF16),
        grad_shape, grad_shape, grad_shape, gw_shape,
    )
    done = pl.pallas_call(
        functools.partial(kernel, heads, views),
        out_shape=tuple(pltpu.VMEM(s.shape, s.dtype) for s in shapes) if PINNED else shapes,
        in_specs=[hbm] * 5 + [smem] * 2,
        out_specs=[vmem] * 5,
        scratch_shapes=scratch,
        compiler_params=pltpu.CompilerParams(
            collective_id=0, has_side_effects=True, vmem_limit_bytes=51 * 1024 * 1024
        ),
        cost_estimate=pl.CostEstimate(
            flops=9_700_000_000, bytes_accessed=18_000_000, transcendentals=2_100_000
        ),
    )(
        queries.reshape(blocks), keys.reshape(blocks), values.reshape(blocks),
        out_grad.reshape(tokens, model), w_out,
        bucket_of.reshape(views, views), pair_mask.reshape(views, views),
    )
    if PINNED:
        done = [pltpu.with_memory_space_constraint(d, pltpu.VMEM) for d in done]
    layer_out, grad_q, grad_k, grad_v, grad_w = pl.pallas_call(
        write_out,
        out_shape=shapes,
        in_specs=[vmem] * 5,
        out_specs=[hbm] * 5,
        scratch_shapes=[dma((5,))],
        compiler_params=pltpu.CompilerParams(vmem_limit_bytes=1024 * 1024),
    )(*done)
    if REDUCE or TIMING:
        grad_w = grad_w.reshape(width, model).astype(BF16)
    else:
        grad_w = lax.psum(grad_w, ("scene", "view")).astype(BF16)
    shape = queries.shape
    return (
        layer_out.reshape(1, 1, tokens, model),
        grad_q.reshape(shape), grad_k.reshape(shape), grad_v.reshape(shape), grad_w,
    )


def solution(mesh):
    split = P("scene", "view", None, None)
    return jax.shard_map(
        body,
        mesh=mesh,
        in_specs=(split, split, split, split, P(), P("scene", None, None), P("scene", None, None)),
        out_specs=(split, split, split, split, P()),
        check_vma=False,
    )
```

```python
import functools
import math

import jax
import jax.numpy as jnp
from jax import lax
from jax.experimental import pallas as pl
from jax.experimental.pallas import tpu as pltpu
from jax.sharding import PartitionSpec as P

HDIM = 128
BLK = 128
NEG_FILL = -1e30
MESH = pl.DeviceIdType.MESH
F32 = jnp.float32
BF16 = jnp.bfloat16
REDUCE = True
TIMING = False
PINNED = True
AHEAD = 2
NT = (((1,), (1,)), ((), ()))
TN = (((0,), (0,)), ((), ()))


def dot(a, b, dims=(((1,), (0,)), ((), ()))):
    return lax.dot_general(a, b, dims, preferred_element_type=F32)


def place(core, y, x, z_hi):
    return ((z_hi * 4 + y) * 4 + x) * 2 + core


def kernel(
    heads,
    views,
    q_hbm, k_hbm, v_hbm, og_hbm, w_hbm, bucket_ref, pair_ref,
    lo_ref, gq_ref, gk_ref, gv_ref, gw_ref,
    qkv_in, og, w, snd, rcv, ga_buf, ga_snd, ga_rcv, mask, wts, gs, gs_t,
    att_snd, att_rcv, att, att_t, g_snd, g_rcv,
    load_sem, big_sem, qs_sem, qr_sem, as_sem, ar_sem, gs_sem, gr_sem, bs_sem, br_sem,
    *reduce_refs,
):
    scene = lax.axis_index("scene")
    me = lax.axis_index("view")
    rows = views * BLK
    inv_root = 1.0 / math.sqrt(HDIM)
    offsets = range(1, views)
    at = [lax.rem(me + o, views) for o in range(views)]
    came = [lax.rem(me + views - o, views) for o in range(views)]

    peers = [(scene, at[o]) for o in offsets]
    if REDUCE:
        part, r0, r1, h1, r2, zsrc, rz, zg, cs, cr, s1s, s1r, s2s, s2r, zs, zr, ts, tr, g2s, g2r, g1s, g1r, gcs, gcr = reduce_refs
        core = lax.rem(scene, 2)
        x = lax.rem(scene // 2, 4)
        y = lax.rem(scene // 8, 4)
        z_hi = scene // 32
        z = z_hi * 4 + me
        first_x = 1 - core
        i1 = first_x * x + core * y
        i2 = first_x * y + core * x
        other = (place(1 - core, y, x, z_hi), me)
        axis1, axis2, along_z = [], [], []
        for o in range(1, 4):
            x1, y1 = lax.rem(x + o * first_x, 4), lax.rem(y + o * core, 4)
            x2, y2 = lax.rem(x + o * core, 4), lax.rem(y + o * first_x, 4)
            axis1.append((place(core, y1, x1, z_hi), me))
            axis2.append((place(core, y2, x2, z_hi), me))
        for o in range(1, 8):
            zz = lax.rem(z + o, 8)
            along_z.append((place(core, y, x, zz // 4), lax.rem(zz, 4)))
        peers = [other] + axis1 + axis2 + along_z

    barrier = pltpu.get_barrier_semaphore()
    for peer in peers:
        pl.semaphore_signal(barrier, inc=1, device_id=peer, device_id_type=MESH)

    loads = []
    for part_id, cols in enumerate((pl.ds(0, HDIM), pl.ds(HDIM, (heads - 1) * HDIM))):
        for t, ref in enumerate((q_hbm, k_hbm, v_hbm)):
            copy = pltpu.make_async_copy(
                ref.at[:, :, cols], qkv_in.at[t, :, :, cols], load_sem.at[t, part_id]
            )
            copy.start()
            loads.append(copy)
    w_load = pltpu.make_async_copy(w_hbm, w, big_sem.at[0])
    og_load = pltpu.make_async_copy(og_hbm, og, big_sem.at[1])
    og_load.start()
    w_load.start()

    block_at = []
    for o in range(views):
        found = jnp.int32(0)
        for j in range(views):
            found = jnp.where(bucket_ref[me, j] == at[o], j, found)
        block_at.append(found)
    lane_view = lax.broadcasted_iota(jnp.int32, (1, rows), 1) // BLK
    for a in range(views):
        row = jnp.zeros((1, rows), F32)
        for b in range(views):
            live = jnp.int32(0)
            for j in range(views):
                live = live + jnp.where(bucket_ref[b, j] == me, 1, 0)
            ok = jnp.where((pair_ref[a, b] > 0) & (live > 0), 1.0, 0.0)
            row = row + jnp.where(lane_view == b, ok, 0.0)
        mask[a] = row

    def cols_of(h, n=1):
        return pl.ds(pl.multiple_of(h * HDIM, HDIM), n * HDIM)

    def qkv_copy(h, o, to):
        slot = at[o] if to else came[o]
        return pltpu.make_async_remote_copy(
            src_ref=snd.at[h, :, at[o]],
            dst_ref=rcv.at[h, :, me if to else slot],
            send_sem=qs_sem.at[h, o],
            recv_sem=qr_sem.at[h, o],
            device_id=(scene, at[o]),
            device_id_type=MESH,
        )

    def ga_copy(h, o, to):
        return pltpu.make_async_remote_copy(
            src_ref=ga_snd.at[h, at[o]],
            dst_ref=ga_rcv.at[h, me if to else came[o]],
            send_sem=as_sem.at[h, o],
            recv_sem=ar_sem.at[h, o],
            device_id=(scene, at[o]),
            device_id_type=MESH,
        )

    def att_copy(h, o, to):
        return pltpu.make_async_remote_copy(
            src_ref=att_snd.at[h, at[o]],
            dst_ref=att_rcv.at[h, me if to else came[o]],
            send_sem=bs_sem.at[h, o],
            recv_sem=br_sem.at[h, o],
            device_id=(scene, at[o]),
            device_id_type=MESH,
        )

    def grad_copy(h, o, to):
        return pltpu.make_async_remote_copy(
            src_ref=g_snd.at[h, :, at[o]],
            dst_ref=g_rcv.at[h, :, me if to else came[o]],
            send_sem=gs_sem.at[h, o],
            recv_sem=gr_sem.at[h, o],
            device_id=(scene, at[o]),
            device_id_type=MESH,
        )

    def pick(which, blocks):
        block = blocks[0]
        for j in range(1, views):
            block = lax.select_n(which == j, block, blocks[j])
        return block

    def pack_qkv(h, carry):
        for t in range(3):
            blocks = [qkv_in[t, j, :, cols_of(h)] for j in range(views)]
            for o in range(views):
                block = pick(block_at[o], blocks)
                if o == 0:
                    rcv[h, t, me] = block
                else:
                    snd[h, t, at[o]] = block
        return carry

    def start_qkv(h):
        for o in offsets:
            qkv_copy(h, o, True).start()

    def start_ga(h):
        for o in offsets:
            ga_copy(h, o, True).start()

    def pack_and_start(h, carry):
        pack_qkv(h, 0)
        start_qkv(h)
        return carry

    for copy in loads[:3]:
        copy.wait()
    pl.semaphore_wait(barrier, len(peers))
    lax.fori_loop(0, 1, pack_and_start, 0)
    for copy in loads[3:]:
        copy.wait()
    lax.fori_loop(1, AHEAD, pack_and_start, 0)
    lax.fori_loop(AHEAD, heads, pack_qkv, 0)

    og_load.wait()
    w_load.wait()

    def make_ga(p, carry):
        ga = dot(og[...], w[pl.ds(pl.multiple_of(p * 2 * HDIM, 2 * HDIM), 2 * HDIM), :], NT)
        ga_buf[:, :, cols_of(2 * p, 2)] = ga.astype(BF16).reshape(views, BLK, 2 * HDIM)
        for s in range(2):
            h = 2 * p + s
            for o in range(views):
                block = ga_buf[block_at[o], :, cols_of(h)]
                if o == 0:
                    ga_rcv[h, me] = block
                else:
                    ga_snd[h, at[o]] = block
        return carry

    lax.fori_loop(0, heads // 2, make_ga, 0)

    def forward(h, more):
        for o in offsets:
            qkv_copy(h, o, False).wait_recv()
        more()
        keys = rcv[h, 1].reshape(rows, HDIM)
        values = rcv[h, 2].reshape(rows, HDIM)
        for o in (1, 2, 3, 0):
            a = at[o]
            scores = dot(rcv[h, 0, a], keys, NT) * inv_root
            scores = jnp.where(mask[a] > 0.5, scores, NEG_FILL)
            peak = jnp.max(scores, axis=1, keepdims=True)
            exponent = jnp.exp(scores - peak)
            weights = exponent * (1.0 / jnp.sum(exponent, axis=1, keepdims=True))
            wts[h, a] = weights
            attended = dot(weights.astype(BF16), values).astype(BF16)
            if o == 0:
                att_rcv[h, me] = attended
            else:
                att_snd[h, a] = attended
                att_copy(h, o, True).start()

    def backward(h, more=None):
        for o in offsets:
            ga_copy(h, o, False).wait_recv()
        if more is not None:
            more()
        keys = rcv[h, 1].reshape(rows, HDIM)
        values = rcv[h, 2].reshape(rows, HDIM)
        for a in range(views):
            weights = wts[h, a]
            grad_weights = dot(ga_rcv[h, a], values, NT)
            row_dot = jnp.sum(weights * grad_weights, axis=1, keepdims=True)
            grad_scores = (weights * (grad_weights - row_dot) * inv_root).astype(BF16)
            gs[pl.ds(a * BLK, BLK), :] = grad_scores
            gs_t[pl.ds(a * BLK, BLK), :] = weights.astype(BF16)
            g_snd[h, 0, a] = dot(grad_scores, keys).astype(BF16)
        queries = rcv[h, 0].reshape(rows, HDIM)
        grads = ga_rcv[h].reshape(rows, HDIM)
        grad_keys = dot(queries, gs[...], TN).T
        g_snd[h, 1] = grad_keys.astype(BF16).reshape(views, BLK, HDIM)
        grad_values = dot(grads, gs_t[...], TN).T
        g_snd[h, 2] = grad_values.astype(BF16).reshape(views, BLK, HDIM)
        for o in offsets:
            grad_copy(h, o, True).start()
        g_rcv[h, :, me] = g_snd[h, :, me]

    home = [bucket_ref[me, j] for j in range(views)]

    def unpack_att(h, carry):
        for o in offsets:
            att_copy(h, o, False).wait_recv()
        blocks = [att_rcv[h, b] for b in range(views)]
        for j in range(views):
            block = pick(home[j], blocks)
            att[pl.ds(j * BLK, BLK), cols_of(h)] = block
            att_t[cols_of(h), pl.ds(j * BLK, BLK)] = block.T
        return carry

    width = heads * HDIM
    wide = 256

    def make_out(c, carry):
        cols = pl.ds(pl.multiple_of(c * wide, wide), wide)
        lo_ref[:, cols] = dot(att[...], w[:, cols]).astype(BF16)
        return carry

    quarter = width // 4

    def make_part(p):
        def step(c, carry):
            rows_in = pl.ds(pl.multiple_of((p * 2 + c) * quarter, quarter), quarter)
            for d in range(og.shape[1] // 512):
                cols = pl.ds(d * 512, 512)
                term = dot(att_t[rows_in, :], og[:, cols])
                if REDUCE:
                    part[p, c, :, cols] = term.astype(BF16)
                else:
                    gw_ref[rows_in, cols] = term
            return carry

        lax.fori_loop(0, 2, step, 0)

    def finish(h, carry):
        for o in offsets:
            grad_copy(h, o, False).wait_recv()
        for t, ref in enumerate((gq_ref, gk_ref, gv_ref)):
            blocks = [g_rcv[h, t, b] for b in range(views)]
            for j in range(views):
                ref[j, :, cols_of(h)] = pick(home[j], blocks)
        for o in offsets:
            qkv_copy(h, o, True).wait_send()
            ga_copy(h, o, True).wait_send()
            att_copy(h, o, True).wait_send()
            grad_copy(h, o, True).wait_send()
        return carry

    def remote(src, dst, s_sem, r_sem, to):
        return pltpu.make_async_remote_copy(
            src_ref=src, dst_ref=dst, send_sem=s_sem, recv_sem=r_sem,
            device_id=to, device_id_type=MESH,
        )

    def rows_of(i, n):
        return pl.ds(pl.multiple_of(i * n, n), n)

    if REDUCE:

        def core_copy(p):
            return remote(part.at[p, 1 - core], r0.at[p], cs.at[p], cr.at[p], other)

        def first_copies(p):
            return [
                remote(
                    part.at[p, core, rows_of(lax.rem(i1 + o, 4), 64)], r1.at[p, o - 1],
                    s1s.at[p, o - 1], s1r.at[p, o - 1], axis1[o - 1],
                )
                for o in range(1, 4)
            ]

        def second_copies(p):
            return [
                remote(
                    h1.at[p, rows_of(lax.rem(i2 + o, 4), 16)], r2.at[p, o - 1],
                    s2s.at[p, o - 1], s2r.at[p, o - 1], axis2[o - 1],
                )
                for o in range(1, 4)
            ]

        def z_copies(p):
            return [
                remote(
                    zsrc.at[p, lax.rem(z + o, 8)], rz.at[p, o - 1],
                    zs.at[p, o - 1], zr.at[p, o - 1], along_z[o - 1],
                )
                for o in range(1, 8)
            ]

        def z_back(p, to):
            spots = [zg.at[p, z if to else lax.rem(z + 8 - o, 8)] for o in range(1, 8)]
            return [
                remote(spots[o], spots[o], ts.at[p, o], tr.at[p, o], along_z[o])
                for o in range(7)
            ]

        def second_back(p, to):
            spots = [
                gw_ref.at[p, core, i1, i2 if to else lax.rem(i2 + 4 - o, 4)] for o in range(1, 4)
            ]
            return [
                remote(spots[o], spots[o], g2s.at[p, o], g2r.at[p, o], axis2[o])
                for o in range(3)
            ]

        def first_back(p, to):
            spots = [
                gw_ref.at[p, core, i1 if to else lax.rem(i1 + 4 - o, 4)] for o in range(1, 4)
            ]
            return [
                remote(spots[o], spots[o], g1s.at[p, o], g1r.at[p, o], axis1[o])
                for o in range(3)
            ]

        def core_back(p, to):
            spot = gw_ref.at[p, core if to else 1 - core]
            return remote(spot, spot, gcs.at[p], gcr.at[p], other)

        def start_all(copies):
            for copy in copies:
                copy.start()

        def wait_all(copies):
            for copy in copies:
                copy.wait()

        def to_first(p):
            core_copy(p).wait()

            def step(i, carry):
                piece = rows_of(i, 32)
                total = part[p, core, piece].astype(F32) + r0[p, piece].astype(F32)
                part[p, core, piece] = total.astype(BF16)
                return carry

            lax.fori_loop(0, quarter // 32, step, 0)
            start_all(first_copies(p))

        def to_second(p):
            wait_all(first_copies(p))
            for i in range(2):
                piece = pl.ds(i * 32, 32)
                mine = pl.ds(pl.multiple_of(i1 * 64 + i * 32, 32), 32)
                total = part[p, core, mine].astype(F32)
                for o in range(3):
                    total = total + r1[p, o, piece].astype(F32)
                h1[p, piece] = total.astype(BF16)
            start_all(second_copies(p))

        def to_z(p):
            wait_all(second_copies(p))
            total = h1[p, rows_of(i2, 16)].astype(F32)
            for o in range(3):
                total = total + r2[p, o].astype(F32)
            total = total.astype(BF16)
            for c in range(8):
                zsrc[p, c] = total[:, c * 256:(c + 1) * 256]
            start_all(z_copies(p))

        def from_z(p):
            wait_all(z_copies(p))
            total = zsrc[p, z].astype(F32)
            for o in range(7):
                total = total + rz[p, o].astype(F32)
            zg[p, z] = total.astype(BF16)
            start_all(z_back(p, True))

        def from_second(p):
            wait_all(z_back(p, False))
            for c in range(8):
                gw_ref[p, core, i1, i2, :, pl.ds(c * 256, 256)] = zg[p, c]
            start_all(second_back(p, True))

        def from_first(p):
            wait_all(second_back(p, False))
            start_all(first_back(p, True))

        def from_core(p):
            wait_all(first_back(p, False))
            core_back(p, True).start()

    def fwd(first, last, more):
        def step(h, carry):
            forward(h, lambda: more(h))
            return carry

        lax.fori_loop(first, last, step, 0)

    def fwd_unpack(first, last, more):
        def step(h, carry):
            forward(h, lambda: more(h))
            unpack_att(h - 2, 0)
            return carry

        lax.fori_loop(first, last, step, 0)

    def next_qkv(h):
        start_qkv(h + AHEAD)

    def next_ga(h):
        start_ga(h + AHEAD - heads)

    def back(first, last):
        def step(h, carry):
            backward(h)
            return carry

        lax.fori_loop(first, last, step, 0)

    def ga_rest(h, carry):
        start_ga(h)
        return carry

    fwd(0, 2, next_qkv)
    fwd_unpack(2, heads - 2, next_qkv)
    make_part(0)
    if REDUCE:
        core_copy(0).start()
    fwd_unpack(heads - 2, heads - 1, next_ga)
    if REDUCE:
        to_first(0)
    fwd_unpack(heads - 1, heads, next_ga)
    lax.fori_loop(AHEAD, heads, ga_rest, 0)
    if REDUCE:
        to_second(0)
    back(0, 1)
    if REDUCE:
        to_z(0)
    lax.fori_loop(heads - 2, heads, unpack_att, 0)
    make_part(1)
    if not REDUCE:
        lax.fori_loop(0, lo_ref.shape[1] // wide, make_out, 0)
        back(1, heads)
        lax.fori_loop(0, heads, finish, 0)
    else:
        core_copy(1).start()
        back(1, 2)
        to_first(1)
        lax.fori_loop(0, lo_ref.shape[1] // wide, make_out, 0)
        back(2, 3)
        from_z(0)
        back(3, 4)
        to_second(1)
        to_z(1)
        from_second(0)
        back(4, 5)
        from_first(0)
        from_z(1)
        back(5, 6)
        from_core(0)
        from_second(1)
        back(6, 7)
        from_first(1)
        back(7, 8)
        lax.fori_loop(0, heads - 4, finish, 0)
        from_core(1)
        lax.fori_loop(heads - 4, heads, finish, 0)
        core_back(0, False).wait()
        core_back(1, False).wait()


def write_out(*refs):
    count = (len(refs) - 1) // 2
    sems = refs[-1]
    copies = [
        pltpu.make_async_copy(refs[i], refs[count + i], sems.at[i]) for i in range(count)
    ]
    for copy in copies:
        copy.start()
    for copy in copies:
        copy.wait()


def body(queries, keys, values, out_grad, w_out, bucket_of, pair_mask):
    views = lax.axis_size("view")
    tokens, width = queries.shape[2:]
    heads = width // HDIM
    model = out_grad.shape[-1]
    rows = views * BLK
    blocks = (views, BLK, width)
    vmem = pl.BlockSpec(memory_space=pltpu.VMEM)
    smem = pl.BlockSpec(memory_space=pltpu.SMEM)
    hbm = pl.BlockSpec(memory_space=pl.ANY)
    dma = pltpu.SemaphoreType.DMA
    scratch = [
        pltpu.VMEM((3,) + blocks, BF16),
        pltpu.VMEM((tokens, model), BF16),
        pltpu.VMEM((width, model), BF16),
        pltpu.VMEM((heads, 3, views, BLK, HDIM), BF16),
        pltpu.VMEM((heads, 3, views, BLK, HDIM), BF16),
        pltpu.VMEM(blocks, BF16),
        pltpu.VMEM((heads, views, BLK, HDIM), BF16),
        pltpu.VMEM((heads, views, BLK, HDIM), BF16),
        pltpu.VMEM((views, 1, rows), F32),
        pltpu.VMEM((heads, views, BLK, rows), F32),
        pltpu.VMEM((rows, rows), BF16),
        pltpu.VMEM((rows, rows), BF16),
        pltpu.VMEM((heads, views, BLK, HDIM), BF16),
        pltpu.VMEM((heads, views, BLK, HDIM), BF16),
        pltpu.VMEM((tokens, width), BF16),
        pltpu.VMEM((width, tokens), BF16),
        pltpu.VMEM((heads, 3, views, BLK, HDIM), BF16),
        pltpu.VMEM((heads, 3, views, BLK, HDIM), BF16),
        dma((3, 2)),
        dma((2,)),
    ] + [dma((heads, views))] * 8
    if REDUCE:
        scratch += [
            pltpu.VMEM((2, 2, width // 4, model), BF16),
            pltpu.VMEM((2, width // 4, model), BF16),
            pltpu.VMEM((2, 3, 64, model), BF16),
            pltpu.VMEM((2, 64, model), BF16),
            pltpu.VMEM((2, 3, 16, model), BF16),
            pltpu.VMEM((2, 8, 16, model // 8), BF16),
            pltpu.VMEM((2, 7, 16, model // 8), BF16),
            pltpu.VMEM((2, 8, 16, model // 8), BF16),
            dma((2,)), dma((2,)),
            dma((2, 3)), dma((2, 3)), dma((2, 3)), dma((2, 3)),
            dma((2, 7)), dma((2, 7)), dma((2, 7)), dma((2, 7)),
            dma((2, 3)), dma((2, 3)), dma((2, 3)), dma((2, 3)),
            dma((2,)), dma((2,)),
        ]
        gw_shape = jax.ShapeDtypeStruct((2, 2, 4, 4, 16, model), BF16)
    else:
        gw_shape = jax.ShapeDtypeStruct((width, model), F32)
    grad_shape = jax.ShapeDtypeStruct(blocks, BF16)
    shapes = (
        jax.ShapeDtypeStruct((tokens, model), BF16),
        grad_shape, grad_shape, grad_shape, gw_shape,
    )
    done = pl.pallas_call(
        functools.partial(kernel, heads, views),
        out_shape=tuple(pltpu.VMEM(s.shape, s.dtype) for s in shapes) if PINNED else shapes,
        in_specs=[hbm] * 5 + [smem] * 2,
        out_specs=[vmem] * 5,
        scratch_shapes=scratch,
        compiler_params=pltpu.CompilerParams(
            collective_id=0, has_side_effects=True, vmem_limit_bytes=51 * 1024 * 1024
        ),
        cost_estimate=pl.CostEstimate(
            flops=9_700_000_000, bytes_accessed=18_000_000, transcendentals=2_100_000
        ),
    )(
        queries.reshape(blocks), keys.reshape(blocks), values.reshape(blocks),
        out_grad.reshape(tokens, model), w_out,
        bucket_of.reshape(views, views), pair_mask.reshape(views, views),
    )
    if PINNED:
        done = [pltpu.with_memory_space_constraint(d, pltpu.VMEM) for d in done]
    layer_out, grad_q, grad_k, grad_v, grad_w = pl.pallas_call(
        write_out,
        out_shape=shapes,
        in_specs=[vmem] * 5,
        out_specs=[hbm] * 5,
        scratch_shapes=[dma((5,))],
        compiler_params=pltpu.CompilerParams(vmem_limit_bytes=1024 * 1024),
    )(*done)
    if REDUCE or TIMING:
        grad_w = grad_w.reshape(width, model).astype(BF16)
    else:
        grad_w = lax.psum(grad_w, ("scene", "view")).astype(BF16)
    shape = queries.shape
    return (
        layer_out.reshape(1, 1, tokens, model),
        grad_q.reshape(shape), grad_k.reshape(shape), grad_v.reshape(shape), grad_w,
    )


def solution(mesh):
    split = P("scene", "view", None, None)
    return jax.shard_map(
        body,
        mesh=mesh,
        in_specs=(split, split, split, split, P(), P("scene", None, None), P("scene", None, None)),
        out_specs=(split, split, split, split, P()),
        check_vma=False,
    )
```

```python
import functools
import math

import jax
import jax.numpy as jnp
from jax import lax
from jax.experimental import pallas as pl
from jax.experimental.pallas import tpu as pltpu
from jax.sharding import PartitionSpec as P

HDIM = 128
BLK = 128
NEG_FILL = -1e30
MESH = pl.DeviceIdType.MESH
F32 = jnp.float32
BF16 = jnp.bfloat16
REDUCE = True
TIMING = False
PINNED = True
NT = (((1,), (1,)), ((), ()))
TN = (((0,), (0,)), ((), ()))


def dot(a, b, dims=(((1,), (0,)), ((), ()))):
    return lax.dot_general(a, b, dims, preferred_element_type=F32)


def place(core, y, x, z_hi):
    return ((z_hi * 4 + y) * 4 + x) * 2 + core


def kernel(
    heads,
    views,
    q_hbm, k_hbm, v_hbm, og_hbm, w_hbm, bucket_ref, pair_ref,
    lo_ref, gq_ref, gk_ref, gv_ref, gw_ref,
    qkv_in, og, w, snd, rcv, ga_buf, ga_snd, ga_rcv, mask, wts, gs, gs_t,
    att_snd, att_rcv, att, att_t, g_snd, g_rcv,
    load_sem, big_sem, qs_sem, qr_sem, as_sem, ar_sem, gs_sem, gr_sem, bs_sem, br_sem,
    *reduce_refs,
):
    scene = lax.axis_index("scene")
    me = lax.axis_index("view")
    rows = views * BLK
    inv_root = 1.0 / math.sqrt(HDIM)
    offsets = range(1, views)
    at = [lax.rem(me + o, views) for o in range(views)]
    came = [lax.rem(me + views - o, views) for o in range(views)]

    peers = [(scene, at[o]) for o in offsets]
    if REDUCE:
        part, gsum, r0, r1, r2, zsrc, rz, zp, zx, zg, cs, cr, s1s, s1r, s2s, s2r, zs, zr, xs, xr, ts, tr, g2s, g2r, g1s, g1r, gcs, gcr = reduce_refs
        core = lax.rem(scene, 2)
        x = lax.rem(scene // 2, 4)
        y = lax.rem(scene // 8, 4)
        z_hi = scene // 32
        z = z_hi * 4 + me
        first_x = 1 - core
        i1 = first_x * x + core * y
        i2 = first_x * y + core * x
        other = (place(1 - core, y, x, z_hi), me)
        axis1, axis2, along_z = [], [], []
        for o in range(1, 4):
            x1, y1 = lax.rem(x + o * first_x, 4), lax.rem(y + o * core, 4)
            x2, y2 = lax.rem(x + o * core, 4), lax.rem(y + o * first_x, 4)
            axis1.append((place(core, y1, x1, z_hi), me))
            axis2.append((place(core, y2, x2, z_hi), me))
        for o in range(1, 8):
            zz = lax.rem(z + o, 8)
            along_z.append((place(core, y, x, zz // 4), lax.rem(zz, 4)))

        ring = lax.rem(z + 2, 8)
        line = ring // 4

        def on_ring(r):
            zz = lax.rem(r + 6, 8)
            return place(core, y, x, zz // 4), lax.rem(zz, 4)

        mine_z = (1 - line) * ring + line * (7 - ring)
        in_line = []
        for o in range(1, 4):
            c = lax.rem(mine_z + o, 4)
            in_line.append(on_ring((1 - line) * c + line * (7 - c)))
        mirror = on_ring(7 - ring)
        peers = [other] + axis1 + axis2 + along_z

    barrier = pltpu.get_barrier_semaphore()
    for peer in peers:
        pl.semaphore_signal(barrier, inc=1, device_id=peer, device_id_type=MESH)

    loads = []
    for part_id, cols in enumerate((pl.ds(0, HDIM), pl.ds(HDIM, (heads - 1) * HDIM))):
        for t, ref in enumerate((q_hbm, k_hbm, v_hbm)):
            copy = pltpu.make_async_copy(
                ref.at[:, :, cols], qkv_in.at[t, :, :, cols], load_sem.at[t, part_id]
            )
            copy.start()
            loads.append(copy)
    w_load = pltpu.make_async_copy(w_hbm, w, big_sem.at[0])
    og_load = pltpu.make_async_copy(og_hbm, og, big_sem.at[1])
    og_load.start()
    w_load.start()

    block_at = []
    for o in range(views):
        found = jnp.int32(0)
        for j in range(views):
            found = jnp.where(bucket_ref[me, j] == at[o], j, found)
        block_at.append(found)
    lane_view = lax.broadcasted_iota(jnp.int32, (1, rows), 1) // BLK
    for a in range(views):
        row = jnp.zeros((1, rows), F32)
        for b in range(views):
            live = jnp.int32(0)
            for j in range(views):
                live = live + jnp.where(bucket_ref[b, j] == me, 1, 0)
            ok = jnp.where((pair_ref[a, b] > 0) & (live > 0), 1.0, 0.0)
            row = row + jnp.where(lane_view == b, ok, 0.0)
        mask[a] = row

    def cols_of(h, n=1):
        return pl.ds(pl.multiple_of(h * HDIM, HDIM), n * HDIM)

    def qkv_copy(h, o, to):
        slot = at[o] if to else came[o]
        return pltpu.make_async_remote_copy(
            src_ref=snd.at[h, :, at[o]],
            dst_ref=rcv.at[h, :, me if to else slot],
            send_sem=qs_sem.at[h, o],
            recv_sem=qr_sem.at[h, o],
            device_id=(scene, at[o]),
            device_id_type=MESH,
        )

    def ga_copy(h, o, to):
        return pltpu.make_async_remote_copy(
            src_ref=ga_snd.at[h, at[o]],
            dst_ref=ga_rcv.at[h, me if to else came[o]],
            send_sem=as_sem.at[h, o],
            recv_sem=ar_sem.at[h, o],
            device_id=(scene, at[o]),
            device_id_type=MESH,
        )

    def att_copy(h, o, to):
        return pltpu.make_async_remote_copy(
            src_ref=att_snd.at[h, at[o]],
            dst_ref=att_rcv.at[h, me if to else came[o]],
            send_sem=bs_sem.at[h, o],
            recv_sem=br_sem.at[h, o],
            device_id=(scene, at[o]),
            device_id_type=MESH,
        )

    def grad_copy(h, o, to):
        return pltpu.make_async_remote_copy(
            src_ref=g_snd.at[h, :, at[o]],
            dst_ref=g_rcv.at[h, :, me if to else came[o]],
            send_sem=gs_sem.at[h, o],
            recv_sem=gr_sem.at[h, o],
            device_id=(scene, at[o]),
            device_id_type=MESH,
        )

    def pick(which, blocks):
        block = blocks[0]
        for j in range(1, views):
            block = lax.select_n(which == j, block, blocks[j])
        return block

    def send_qkv(h, carry):
        for t in range(3):
            blocks = [qkv_in[t, j, :, cols_of(h)] for j in range(views)]
            for o in range(views):
                block = pick(block_at[o], blocks)
                if o == 0:
                    rcv[h, t, me] = block
                else:
                    snd[h, t, at[o]] = block
        for o in offsets:
            qkv_copy(h, o, True).start()
        return carry

    for copy in loads[:3]:
        copy.wait()
    pl.semaphore_wait(barrier, len(peers))
    lax.fori_loop(0, 1, send_qkv, 0)
    for copy in loads[3:]:
        copy.wait()
    lax.fori_loop(1, heads, send_qkv, 0)

    og_load.wait()
    w_load.wait()

    def make_ga(p, carry):
        ga = dot(og[...], w[pl.ds(pl.multiple_of(p * 2 * HDIM, 2 * HDIM), 2 * HDIM), :], NT)
        ga_buf[:, :, cols_of(2 * p, 2)] = ga.astype(BF16).reshape(views, BLK, 2 * HDIM)
        for s in range(2):
            h = 2 * p + s
            for o in range(views):
                block = ga_buf[block_at[o], :, cols_of(h)]
                if o == 0:
                    ga_rcv[h, me] = block
                else:
                    ga_snd[h, at[o]] = block
        return carry

    lax.fori_loop(0, heads // 2, make_ga, 0)

    def forward(h, carry):
        for o in offsets:
            qkv_copy(h, o, False).wait_recv()
        keys = rcv[h, 1].reshape(rows, HDIM)
        values = rcv[h, 2].reshape(rows, HDIM)
        for o in (1, 2, 3, 0):
            a = at[o]
            scores = dot(rcv[h, 0, a], keys, NT) * inv_root
            scores = jnp.where(mask[a] > 0.5, scores, NEG_FILL)
            peak = jnp.max(scores, axis=1, keepdims=True)
            exponent = jnp.exp(scores - peak)
            weights = exponent * (1.0 / jnp.sum(exponent, axis=1, keepdims=True))
            wts[h, a] = weights
            attended = dot(weights.astype(BF16), values).astype(BF16)
            if o == 0:
                att_rcv[h, me] = attended
            else:
                att_snd[h, a] = attended
                att_copy(h, o, True).start()
        return carry

    lax.fori_loop(0, heads, forward, 0)

    def send_ga(h, carry):
        for o in offsets:
            ga_copy(h, o, True).start()
        return carry

    lax.fori_loop(0, heads, send_ga, 0)

    def backward(h, carry):
        for o in offsets:
            ga_copy(h, o, False).wait_recv()
        keys = rcv[h, 1].reshape(rows, HDIM)
        values = rcv[h, 2].reshape(rows, HDIM)
        for a in range(views):
            weights = wts[h, a]
            grad_weights = dot(ga_rcv[h, a], values, NT)
            row_dot = jnp.sum(weights * grad_weights, axis=1, keepdims=True)
            grad_scores = (weights * (grad_weights - row_dot) * inv_root).astype(BF16)
            gs[pl.ds(a * BLK, BLK), :] = grad_scores
            gs_t[pl.ds(a * BLK, BLK), :] = weights.astype(BF16)
            g_snd[h, 0, a] = dot(grad_scores, keys).astype(BF16)
        queries = rcv[h, 0].reshape(rows, HDIM)
        grads = ga_rcv[h].reshape(rows, HDIM)
        grad_keys = dot(queries, gs[...], TN).T
        g_snd[h, 1] = grad_keys.astype(BF16).reshape(views, BLK, HDIM)
        grad_values = dot(grads, gs_t[...], TN).T
        g_snd[h, 2] = grad_values.astype(BF16).reshape(views, BLK, HDIM)
        for o in offsets:
            grad_copy(h, o, True).start()
        g_rcv[h, :, me] = g_snd[h, :, me]
        return carry

    home = [bucket_ref[me, j] for j in range(views)]

    def unpack_att(h, carry):
        for o in offsets:
            att_copy(h, o, False).wait_recv()
        blocks = [att_rcv[h, b] for b in range(views)]
        for j in range(views):
            block = pick(home[j], blocks)
            att[pl.ds(j * BLK, BLK), cols_of(h)] = block
            att_t[cols_of(h), pl.ds(j * BLK, BLK)] = block.T
        return carry

    width = heads * HDIM
    wide = 256

    def make_out(c, carry):
        cols = pl.ds(pl.multiple_of(c * wide, wide), wide)
        lo_ref[:, cols] = dot(att[...], w[:, cols]).astype(BF16)
        return carry

    def make_part(c, carry):
        span = pl.ds(pl.multiple_of(c * wide, wide), wide)
        for d in range(og.shape[1] // 512):
            cols = pl.ds(d * 512, 512)
            term = dot(att_t[span, :], og[:, cols])
            if REDUCE:
                part[span, cols] = term.astype(BF16)
            else:
                gw_ref[span, cols] = term
        return carry

    lax.fori_loop(0, heads, unpack_att, 0)
    lax.fori_loop(0, width // wide, make_part, 0)
    if REDUCE:
        half = width // 2
        core_rows = pl.ds(pl.multiple_of(core * half, half), half)
        other_rows = pl.ds(pl.multiple_of((1 - core) * half, half), half)

        def remote(src, dst, s_sem, r_sem, to):
            return pltpu.make_async_remote_copy(
                src_ref=src, dst_ref=dst, send_sem=s_sem, recv_sem=r_sem,
                device_id=to, device_id_type=MESH,
            )

        c_copy = remote(part.at[other_rows], r0, cs, cr, other)
        c_copy.start()
    lax.fori_loop(0, lo_ref.shape[1] // wide, make_out, 0)

    if not REDUCE:
        lax.fori_loop(0, heads, backward, 0)
    else:
        lax.fori_loop(0, 1, backward, 0)
        c_copy.wait()

        def sum_core(i, carry):
            piece = pl.ds(pl.multiple_of(i * 32, 32), 32)
            mine = pl.ds(pl.multiple_of(core * half + i * 32, 32), 32)
            gsum[piece] = (part[mine].astype(F32) + r0[piece].astype(F32)).astype(BF16)
            return carry

        lax.fori_loop(0, half // 32, sum_core, 0)

        def rows_of(i, n):
            return pl.ds(pl.multiple_of(i * n, n), n)

        rs1 = [
            remote(gsum.at[rows_of(lax.rem(i1 + o, 4), 128)], r1.at[o - 1], s1s.at[o - 1], s1r.at[o - 1], axis1[o - 1])
            for o in range(1, 4)
        ]
        for copy in rs1:
            copy.start()
        lax.fori_loop(1, 2, backward, 0)
        for copy in rs1:
            copy.wait()

        def sum_1(i, carry):
            piece = pl.ds(pl.multiple_of(i * 32, 32), 32)
            total = gsum[pl.ds(pl.multiple_of(i1 * 128 + i * 32, 32), 32)].astype(F32)
            for o in range(3):
                total = total + r1[o, piece].astype(F32)
            r0[piece] = total.astype(BF16)
            return carry

        lax.fori_loop(0, 4, sum_1, 0)
        rs2 = [
            remote(r0.at[rows_of(lax.rem(i2 + o, 4), 32)], r2.at[o - 1], s2s.at[o - 1], s2r.at[o - 1], axis2[o - 1])
            for o in range(1, 4)
        ]
        for copy in rs2:
            copy.start()
        for copy in rs2:
            copy.wait()
        total = r0[rows_of(i2, 32)].astype(F32)
        for o in range(3):
            total = total + r2[o].astype(F32)
        total = total.astype(BF16)
        for p in range(4):
            zsrc[p] = total[:, p * 512:(p + 1) * 512]
        rsz = [
            remote(zsrc.at[lax.rem(mine_z + o, 4)], rz.at[o - 1], zs.at[o - 1], zr.at[o - 1], in_line[o - 1])
            for o in range(1, 4)
        ]
        for copy in rsz:
            copy.start()
        lax.fori_loop(2, 3, backward, 0)
        for copy in rsz:
            copy.wait()
        total = zsrc[mine_z].astype(F32)
        for o in range(3):
            total = total + rz[o].astype(F32)
        zp[...] = total.astype(BF16)
        across = remote(zp, zx, xs, xr, mirror)
        across.start()
        lax.fori_loop(3, 4, backward, 0)
        across.wait()
        zg[mine_z] = (zp[...].astype(F32) + zx[...].astype(F32)).astype(BF16)
        for o in range(1, 4):
            spot = zg.at[mine_z]
            remote(spot, spot, ts.at[o - 1], tr.at[o - 1], in_line[o - 1]).start()
        lax.fori_loop(4, 5, backward, 0)
        for o in range(1, 4):
            spot = zg.at[lax.rem(mine_z + 4 - o, 4)]
            remote(spot, spot, ts.at[o - 1], tr.at[o - 1], in_line[o - 1]).wait()
        for p in range(4):
            gw_ref[core, i1, i2, :, pl.ds(p * 512, 512)] = zg[p]
        for o in range(1, 4):
            spot = gw_ref.at[core, i1, i2]
            remote(spot, spot, g2s.at[o - 1], g2r.at[o - 1], axis2[o - 1]).start()
        lax.fori_loop(5, 6, backward, 0)
        for o in range(1, 4):
            spot = gw_ref.at[core, i1, lax.rem(i2 + 4 - o, 4)]
            remote(spot, spot, g2s.at[o - 1], g2r.at[o - 1], axis2[o - 1]).wait()
        for o in range(1, 4):
            spot = gw_ref.at[core, i1]
            remote(spot, spot, g1s.at[o - 1], g1r.at[o - 1], axis1[o - 1]).start()
        lax.fori_loop(6, heads, backward, 0)
        for o in range(1, 4):
            spot = gw_ref.at[core, lax.rem(i1 + 4 - o, 4)]
            remote(spot, spot, g1s.at[o - 1], g1r.at[o - 1], axis1[o - 1]).wait()
        spot = gw_ref.at[core]
        remote(spot, spot, gcs, gcr, other).start()

    def finish(h, carry):
        for o in offsets:
            grad_copy(h, o, False).wait_recv()
        for t, ref in enumerate((gq_ref, gk_ref, gv_ref)):
            blocks = [g_rcv[h, t, b] for b in range(views)]
            for j in range(views):
                ref[j, :, cols_of(h)] = pick(home[j], blocks)
        for o in offsets:
            qkv_copy(h, o, True).wait_send()
            ga_copy(h, o, True).wait_send()
            att_copy(h, o, True).wait_send()
            grad_copy(h, o, True).wait_send()
        return carry

    lax.fori_loop(0, heads, finish, 0)
    if REDUCE:
        spot = gw_ref.at[1 - core]
        remote(spot, spot, gcs, gcr, other).wait()


def write_out(*refs):
    count = (len(refs) - 1) // 2
    sems = refs[-1]
    copies = [
        pltpu.make_async_copy(refs[i], refs[count + i], sems.at[i]) for i in range(count)
    ]
    for copy in copies:
        copy.start()
    for copy in copies:
        copy.wait()


def body(queries, keys, values, out_grad, w_out, bucket_of, pair_mask):
    views = lax.axis_size("view")
    tokens, width = queries.shape[2:]
    heads = width // HDIM
    model = out_grad.shape[-1]
    rows = views * BLK
    blocks = (views, BLK, width)
    vmem = pl.BlockSpec(memory_space=pltpu.VMEM)
    smem = pl.BlockSpec(memory_space=pltpu.SMEM)
    hbm = pl.BlockSpec(memory_space=pl.ANY)
    dma = pltpu.SemaphoreType.DMA
    scratch = [
        pltpu.VMEM((3,) + blocks, BF16),
        pltpu.VMEM((tokens, model), BF16),
        pltpu.VMEM((width, model), BF16),
        pltpu.VMEM((heads, 3, views, BLK, HDIM), BF16),
        pltpu.VMEM((heads, 3, views, BLK, HDIM), BF16),
        pltpu.VMEM(blocks, BF16),
        pltpu.VMEM((heads, views, BLK, HDIM), BF16),
        pltpu.VMEM((heads, views, BLK, HDIM), BF16),
        pltpu.VMEM((views, 1, rows), F32),
        pltpu.VMEM((heads, views, BLK, rows), F32),
        pltpu.VMEM((rows, rows), BF16),
        pltpu.VMEM((rows, rows), BF16),
        pltpu.VMEM((heads, views, BLK, HDIM), BF16),
        pltpu.VMEM((heads, views, BLK, HDIM), BF16),
        pltpu.VMEM((tokens, width), BF16),
        pltpu.VMEM((width, tokens), BF16),
        pltpu.VMEM((heads, 3, views, BLK, HDIM), BF16),
        pltpu.VMEM((heads, 3, views, BLK, HDIM), BF16),
        dma((3, 2)),
        dma((2,)),
    ] + [dma((heads, views))] * 8
    if REDUCE:
        scratch += [
            pltpu.VMEM((width, model), BF16),
            pltpu.VMEM((width // 2, model), BF16),
            pltpu.VMEM((width // 2, model), BF16),
            pltpu.VMEM((3, 128, model), BF16),
            pltpu.VMEM((3, 32, model), BF16),
            pltpu.VMEM((4, 32, model // 4), BF16),
            pltpu.VMEM((3, 32, model // 4), BF16),
            pltpu.VMEM((32, model // 4), BF16),
            pltpu.VMEM((32, model // 4), BF16),
            pltpu.VMEM((4, 32, model // 4), BF16),
            dma, dma,
            dma((3,)), dma((3,)), dma((3,)), dma((3,)),
            dma((3,)), dma((3,)), dma, dma, dma((3,)), dma((3,)),
            dma((3,)), dma((3,)), dma((3,)), dma((3,)),
            dma, dma,
        ]
        gw_shape = jax.ShapeDtypeStruct((2, 4, 4, 32, model), BF16)
    else:
        gw_shape = jax.ShapeDtypeStruct((width, model), F32)
    grad_shape = jax.ShapeDtypeStruct(blocks, BF16)
    shapes = (
        jax.ShapeDtypeStruct((tokens, model), BF16),
        grad_shape, grad_shape, grad_shape, gw_shape,
    )
    done = pl.pallas_call(
        functools.partial(kernel, heads, views),
        out_shape=tuple(pltpu.VMEM(s.shape, s.dtype) for s in shapes) if PINNED else shapes,
        in_specs=[hbm] * 5 + [smem] * 2,
        out_specs=[vmem] * 5,
        scratch_shapes=scratch,
        compiler_params=pltpu.CompilerParams(
            collective_id=0, has_side_effects=True, vmem_limit_bytes=51 * 1024 * 1024
        ),
        cost_estimate=pl.CostEstimate(
            flops=9_700_000_000, bytes_accessed=18_000_000, transcendentals=2_100_000
        ),
    )(
        queries.reshape(blocks), keys.reshape(blocks), values.reshape(blocks),
        out_grad.reshape(tokens, model), w_out,
        bucket_of.reshape(views, views), pair_mask.reshape(views, views),
    )
    if PINNED:
        done = [pltpu.with_memory_space_constraint(d, pltpu.VMEM) for d in done]
    layer_out, grad_q, grad_k, grad_v, grad_w = pl.pallas_call(
        write_out,
        out_shape=shapes,
        in_specs=[vmem] * 5,
        out_specs=[hbm] * 5,
        scratch_shapes=[dma((5,))],
        compiler_params=pltpu.CompilerParams(vmem_limit_bytes=1024 * 1024),
    )(*done)
    if REDUCE or TIMING:
        grad_w = grad_w.reshape(width, model).astype(BF16)
    else:
        grad_w = lax.psum(grad_w, ("scene", "view")).astype(BF16)
    shape = queries.shape
    return (
        layer_out.reshape(1, 1, tokens, model),
        grad_q.reshape(shape), grad_k.reshape(shape), grad_v.reshape(shape), grad_w,
    )


def solution(mesh):
    split = P("scene", "view", None, None)
    return jax.shard_map(
        body,
        mesh=mesh,
        in_specs=(split, split, split, split, P(), P("scene", None, None), P("scene", None, None)),
        out_specs=(split, split, split, split, P()),
        check_vma=False,
    )
```

```python
import functools
import math

import jax
import jax.numpy as jnp
from jax import lax
from jax.experimental import pallas as pl
from jax.experimental.pallas import tpu as pltpu
from jax.sharding import PartitionSpec as P

HDIM = 128
BLK = 128
NEG_FILL = -1e30
MESH = pl.DeviceIdType.MESH
F32 = jnp.float32
BF16 = jnp.bfloat16
REDUCE = True
TIMING = False
PINNED = True
NT = (((1,), (1,)), ((), ()))
TN = (((0,), (0,)), ((), ()))


def dot(a, b, dims=(((1,), (0,)), ((), ()))):
    return lax.dot_general(a, b, dims, preferred_element_type=F32)


def place(core, y, x, z_hi):
    return ((z_hi * 4 + y) * 4 + x) * 2 + core


def kernel(
    heads,
    views,
    q_hbm, k_hbm, v_hbm, og_hbm, w_hbm, bucket_ref, pair_ref,
    lo_ref, gq_ref, gk_ref, gv_ref, gw_ref,
    qkv_in, og, w, snd, rcv, ga_buf, ga_snd, ga_rcv, mask, wts, gs, gs_t,
    att_snd, att_rcv, att, att_t, g_snd, g_rcv,
    load_sem, big_sem, qs_sem, qr_sem, as_sem, ar_sem, gs_sem, gr_sem, bs_sem, br_sem,
    *reduce_refs,
):
    scene = lax.axis_index("scene")
    me = lax.axis_index("view")
    rows = views * BLK
    inv_root = 1.0 / math.sqrt(HDIM)
    offsets = range(1, views)
    at = [lax.rem(me + o, views) for o in range(views)]
    came = [lax.rem(me + views - o, views) for o in range(views)]

    peers = [(scene, at[o]) for o in offsets]
    if REDUCE:
        part, gsum, r0, r1, r2, zsrc, rz, zp, zx, zg, cs, cr, s1s, s1r, s2s, s2r, zs, zr, xs, xr, ts, tr, g2s, g2r, g1s, g1r, gcs, gcr = reduce_refs
        core = lax.rem(scene, 2)
        x = lax.rem(scene // 2, 4)
        y = lax.rem(scene // 8, 4)
        z_hi = scene // 32
        z = z_hi * 4 + me
        first_x = 1 - core
        i1 = first_x * x + core * y
        i2 = first_x * y + core * x
        other = (place(1 - core, y, x, z_hi), me)
        axis1, axis2, along_z = [], [], []
        for o in range(1, 4):
            x1, y1 = lax.rem(x + o * first_x, 4), lax.rem(y + o * core, 4)
            x2, y2 = lax.rem(x + o * core, 4), lax.rem(y + o * first_x, 4)
            axis1.append((place(core, y1, x1, z_hi), me))
            axis2.append((place(core, y2, x2, z_hi), me))
        for o in range(1, 8):
            zz = lax.rem(z + o, 8)
            along_z.append((place(core, y, x, zz // 4), lax.rem(zz, 4)))

        ring = lax.rem(z + 2, 8)
        line = ring // 4

        def on_ring(r):
            zz = lax.rem(r + 6, 8)
            return place(core, y, x, zz // 4), lax.rem(zz, 4)

        mine_z = (1 - line) * ring + line * (7 - ring)
        in_line = []
        for o in range(1, 4):
            c = lax.rem(mine_z + o, 4)
            in_line.append(on_ring((1 - line) * c + line * (7 - c)))
        mirror = on_ring(7 - ring)
        peers = [other] + axis1 + axis2 + along_z

    barrier = pltpu.get_barrier_semaphore()
    for peer in peers:
        pl.semaphore_signal(barrier, inc=1, device_id=peer, device_id_type=MESH)

    loads = []
    for part_id, cols in enumerate((pl.ds(0, HDIM), pl.ds(HDIM, (heads - 1) * HDIM))):
        for t, ref in enumerate((q_hbm, k_hbm, v_hbm)):
            copy = pltpu.make_async_copy(
                ref.at[:, :, cols], qkv_in.at[t, :, :, cols], load_sem.at[t, part_id]
            )
            copy.start()
            loads.append(copy)
    w_load = pltpu.make_async_copy(w_hbm, w, big_sem.at[0])
    og_load = pltpu.make_async_copy(og_hbm, og, big_sem.at[1])
    og_load.start()
    w_load.start()

    block_at = []
    for o in range(views):
        found = jnp.int32(0)
        for j in range(views):
            found = jnp.where(bucket_ref[me, j] == at[o], j, found)
        block_at.append(found)
    lane_view = lax.broadcasted_iota(jnp.int32, (1, rows), 1) // BLK
    for a in range(views):
        row = jnp.zeros((1, rows), F32)
        for b in range(views):
            live = jnp.int32(0)
            for j in range(views):
                live = live + jnp.where(bucket_ref[b, j] == me, 1, 0)
            ok = jnp.where((pair_ref[a, b] > 0) & (live > 0), 1.0, 0.0)
            row = row + jnp.where(lane_view == b, ok, 0.0)
        mask[a] = row

    def cols_of(h, n=1):
        return pl.ds(pl.multiple_of(h * HDIM, HDIM), n * HDIM)

    def qkv_copy(h, o, to):
        slot = at[o] if to else came[o]
        return pltpu.make_async_remote_copy(
            src_ref=snd.at[h, :, at[o]],
            dst_ref=rcv.at[h, :, me if to else slot],
            send_sem=qs_sem.at[h, o],
            recv_sem=qr_sem.at[h, o],
            device_id=(scene, at[o]),
            device_id_type=MESH,
        )

    def ga_copy(h, o, to):
        return pltpu.make_async_remote_copy(
            src_ref=ga_snd.at[h, at[o]],
            dst_ref=ga_rcv.at[h, me if to else came[o]],
            send_sem=as_sem.at[h, o],
            recv_sem=ar_sem.at[h, o],
            device_id=(scene, at[o]),
            device_id_type=MESH,
        )

    def att_copy(h, o, to):
        return pltpu.make_async_remote_copy(
            src_ref=att_snd.at[h, at[o]],
            dst_ref=att_rcv.at[h, me if to else came[o]],
            send_sem=bs_sem.at[h, o],
            recv_sem=br_sem.at[h, o],
            device_id=(scene, at[o]),
            device_id_type=MESH,
        )

    def grad_copy(h, o, to):
        return pltpu.make_async_remote_copy(
            src_ref=g_snd.at[h, :, at[o]],
            dst_ref=g_rcv.at[h, :, me if to else came[o]],
            send_sem=gs_sem.at[h, o],
            recv_sem=gr_sem.at[h, o],
            device_id=(scene, at[o]),
            device_id_type=MESH,
        )

    def pick(which, blocks):
        block = blocks[0]
        for j in range(1, views):
            block = lax.select_n(which == j, block, blocks[j])
        return block

    def send_qkv(h, carry):
        for t in range(3):
            blocks = [qkv_in[t, j, :, cols_of(h)] for j in range(views)]
            for o in range(views):
                block = pick(block_at[o], blocks)
                if o == 0:
                    rcv[h, t, me] = block
                else:
                    snd[h, t, at[o]] = block
        for o in offsets:
            qkv_copy(h, o, True).start()
        return carry

    for copy in loads[:3]:
        copy.wait()
    pl.semaphore_wait(barrier, len(peers))
    lax.fori_loop(0, 1, send_qkv, 0)
    for copy in loads[3:]:
        copy.wait()
    lax.fori_loop(1, heads, send_qkv, 0)

    og_load.wait()
    w_load.wait()

    def make_ga(p, carry):
        ga = dot(og[...], w[pl.ds(pl.multiple_of(p * 2 * HDIM, 2 * HDIM), 2 * HDIM), :], NT)
        ga_buf[:, :, cols_of(2 * p, 2)] = ga.astype(BF16).reshape(views, BLK, 2 * HDIM)
        for s in range(2):
            h = 2 * p + s
            for o in range(views):
                block = ga_buf[block_at[o], :, cols_of(h)]
                if o == 0:
                    ga_rcv[h, me] = block
                else:
                    ga_snd[h, at[o]] = block
        return carry

    lax.fori_loop(0, heads // 2, make_ga, 0)

    def forward(h, carry):
        for o in offsets:
            qkv_copy(h, o, False).wait_recv()
        keys = rcv[h, 1].reshape(rows, HDIM)
        values = rcv[h, 2].reshape(rows, HDIM)
        for o in (1, 2, 3, 0):
            a = at[o]
            scores = dot(rcv[h, 0, a], keys, NT) * inv_root
            scores = jnp.where(mask[a] > 0.5, scores, NEG_FILL)
            peak = jnp.max(scores, axis=1, keepdims=True)
            exponent = jnp.exp(scores - peak)
            weights = exponent * (1.0 / jnp.sum(exponent, axis=1, keepdims=True))
            wts[h, a] = weights
            attended = dot(weights.astype(BF16), values).astype(BF16)
            if o == 0:
                att_rcv[h, me] = attended
            else:
                att_snd[h, a] = attended
                att_copy(h, o, True).start()
        return carry

    lax.fori_loop(0, heads, forward, 0)

    def send_ga(h, carry):
        for o in offsets:
            ga_copy(h, o, True).start()
        return carry

    lax.fori_loop(0, heads, send_ga, 0)

    def backward(h, carry):
        for o in offsets:
            ga_copy(h, o, False).wait_recv()
        keys = rcv[h, 1].reshape(rows, HDIM)
        values = rcv[h, 2].reshape(rows, HDIM)
        for a in range(views):
            weights = wts[h, a]
            grad_weights = dot(ga_rcv[h, a], values, NT)
            row_dot = jnp.sum(weights * grad_weights, axis=1, keepdims=True)
            grad_scores = (weights * (grad_weights - row_dot) * inv_root).astype(BF16)
            gs[pl.ds(a * BLK, BLK), :] = grad_scores
            gs_t[pl.ds(a * BLK, BLK), :] = weights.astype(BF16)
            g_snd[h, 0, a] = dot(grad_scores, keys).astype(BF16)
        queries = rcv[h, 0].reshape(rows, HDIM)
        grads = ga_rcv[h].reshape(rows, HDIM)
        grad_keys = dot(queries, gs[...], TN).T
        g_snd[h, 1] = grad_keys.astype(BF16).reshape(views, BLK, HDIM)
        grad_values = dot(grads, gs_t[...], TN).T
        g_snd[h, 2] = grad_values.astype(BF16).reshape(views, BLK, HDIM)
        for o in offsets:
            grad_copy(h, o, True).start()
        g_rcv[h, :, me] = g_snd[h, :, me]
        return carry

    home = [bucket_ref[me, j] for j in range(views)]

    def unpack_att(h, carry):
        for o in offsets:
            att_copy(h, o, False).wait_recv()
        blocks = [att_rcv[h, b] for b in range(views)]
        for j in range(views):
            block = pick(home[j], blocks)
            att[pl.ds(j * BLK, BLK), cols_of(h)] = block
            att_t[cols_of(h), pl.ds(j * BLK, BLK)] = block.T
        return carry

    width = heads * HDIM
    wide = 256

    def make_out(c, carry):
        cols = pl.ds(pl.multiple_of(c * wide, wide), wide)
        lo_ref[:, cols] = dot(att[...], w[:, cols]).astype(BF16)
        return carry

    first_half = 1 - lax.rem(scene, 2)

    def make_part(c, carry):
        half_at = lax.rem(first_half + c // 2, 2)
        span = pl.ds(pl.multiple_of((half_at * 2 + lax.rem(c, 2)) * wide, wide), wide)
        for d in range(og.shape[1] // 512):
            cols = pl.ds(d * 512, 512)
            term = dot(att_t[span, :], og[:, cols])
            if REDUCE:
                part[span, cols] = term.astype(BF16)
            else:
                gw_ref[span, cols] = term
        return carry

    lax.fori_loop(0, heads, unpack_att, 0)
    lax.fori_loop(0, 2, make_part, 0)
    if REDUCE:
        half = width // 2
        core_rows = pl.ds(pl.multiple_of(core * half, half), half)
        other_rows = pl.ds(pl.multiple_of((1 - core) * half, half), half)

        def remote(src, dst, s_sem, r_sem, to):
            return pltpu.make_async_remote_copy(
                src_ref=src, dst_ref=dst, send_sem=s_sem, recv_sem=r_sem,
                device_id=to, device_id_type=MESH,
            )

        c_copy = remote(part.at[other_rows], r0, cs, cr, other)
        c_copy.start()
    lax.fori_loop(2, 4, make_part, 0)

    if not REDUCE:
        lax.fori_loop(0, lo_ref.shape[1] // wide, make_out, 0)
        lax.fori_loop(0, heads, backward, 0)
    else:
        lax.fori_loop(0, 1, backward, 0)
        c_copy.wait()

        def sum_core(i, carry):
            piece = pl.ds(pl.multiple_of(i * 32, 32), 32)
            mine = pl.ds(pl.multiple_of(core * half + i * 32, 32), 32)
            gsum[piece] = (part[mine].astype(F32) + r0[piece].astype(F32)).astype(BF16)
            return carry

        lax.fori_loop(0, half // 32, sum_core, 0)

        def rows_of(i, n):
            return pl.ds(pl.multiple_of(i * n, n), n)

        rs1 = [
            remote(gsum.at[rows_of(lax.rem(i1 + o, 4), 128)], r1.at[o - 1], s1s.at[o - 1], s1r.at[o - 1], axis1[o - 1])
            for o in range(1, 4)
        ]
        for copy in rs1:
            copy.start()
        lax.fori_loop(1, 2, backward, 0)
        lax.fori_loop(0, lo_ref.shape[1] // wide, make_out, 0)
        for copy in rs1:
            copy.wait()

        def sum_1(i, carry):
            piece = pl.ds(pl.multiple_of(i * 32, 32), 32)
            total = gsum[pl.ds(pl.multiple_of(i1 * 128 + i * 32, 32), 32)].astype(F32)
            for o in range(3):
                total = total + r1[o, piece].astype(F32)
            r0[piece] = total.astype(BF16)
            return carry

        lax.fori_loop(0, 4, sum_1, 0)
        rs2 = [
            remote(r0.at[rows_of(lax.rem(i2 + o, 4), 32)], r2.at[o - 1], s2s.at[o - 1], s2r.at[o - 1], axis2[o - 1])
            for o in range(1, 4)
        ]
        for copy in rs2:
            copy.start()
        for copy in rs2:
            copy.wait()
        total = r0[rows_of(i2, 32)].astype(F32)
        for o in range(3):
            total = total + r2[o].astype(F32)
        total = total.astype(BF16)
        for p in range(4):
            zsrc[p] = total[:, p * 512:(p + 1) * 512]
        rsz = [
            remote(zsrc.at[lax.rem(mine_z + o, 4)], rz.at[o - 1], zs.at[o - 1], zr.at[o - 1], in_line[o - 1])
            for o in range(1, 4)
        ]
        for copy in rsz:
            copy.start()
        lax.fori_loop(2, 3, backward, 0)
        for copy in rsz:
            copy.wait()
        total = zsrc[mine_z].astype(F32)
        for o in range(3):
            total = total + rz[o].astype(F32)
        zp[...] = total.astype(BF16)
        across = remote(zp, zx, xs, xr, mirror)
        across.start()
        lax.fori_loop(3, 4, backward, 0)
        across.wait()
        zg[mine_z] = (zp[...].astype(F32) + zx[...].astype(F32)).astype(BF16)
        for o in range(1, 4):
            spot = zg.at[mine_z]
            remote(spot, spot, ts.at[o - 1], tr.at[o - 1], in_line[o - 1]).start()
        lax.fori_loop(4, 5, backward, 0)
        for o in range(1, 4):
            spot = zg.at[lax.rem(mine_z + 4 - o, 4)]
            remote(spot, spot, ts.at[o - 1], tr.at[o - 1], in_line[o - 1]).wait()
        for p in range(4):
            gw_ref[core, i1, i2, :, pl.ds(p * 512, 512)] = zg[p]
        for o in range(1, 4):
            spot = gw_ref.at[core, i1, i2]
            remote(spot, spot, g2s.at[o - 1], g2r.at[o - 1], axis2[o - 1]).start()
        lax.fori_loop(5, 6, backward, 0)
        for o in range(1, 4):
            spot = gw_ref.at[core, i1, lax.rem(i2 + 4 - o, 4)]
            remote(spot, spot, g2s.at[o - 1], g2r.at[o - 1], axis2[o - 1]).wait()
        for o in range(1, 4):
            spot = gw_ref.at[core, i1]
            remote(spot, spot, g1s.at[o - 1], g1r.at[o - 1], axis1[o - 1]).start()
        lax.fori_loop(6, heads, backward, 0)
        for o in range(1, 4):
            spot = gw_ref.at[core, lax.rem(i1 + 4 - o, 4)]
            remote(spot, spot, g1s.at[o - 1], g1r.at[o - 1], axis1[o - 1]).wait()
        spot = gw_ref.at[core]
        remote(spot, spot, gcs, gcr, other).start()

    def finish(h, carry):
        for o in offsets:
            grad_copy(h, o, False).wait_recv()
        for t, ref in enumerate((gq_ref, gk_ref, gv_ref)):
            blocks = [g_rcv[h, t, b] for b in range(views)]
            for j in range(views):
                ref[j, :, cols_of(h)] = pick(home[j], blocks)
        for o in offsets:
            qkv_copy(h, o, True).wait_send()
            ga_copy(h, o, True).wait_send()
            att_copy(h, o, True).wait_send()
            grad_copy(h, o, True).wait_send()
        return carry

    lax.fori_loop(0, heads, finish, 0)
    if REDUCE:
        spot = gw_ref.at[1 - core]
        remote(spot, spot, gcs, gcr, other).wait()


def write_out(*refs):
    count = (len(refs) - 1) // 2
    sems = refs[-1]
    copies = [
        pltpu.make_async_copy(refs[i], refs[count + i], sems.at[i]) for i in range(count)
    ]
    for copy in copies:
        copy.start()
    for copy in copies:
        copy.wait()


def body(queries, keys, values, out_grad, w_out, bucket_of, pair_mask):
    views = lax.axis_size("view")
    tokens, width = queries.shape[2:]
    heads = width // HDIM
    model = out_grad.shape[-1]
    rows = views * BLK
    blocks = (views, BLK, width)
    vmem = pl.BlockSpec(memory_space=pltpu.VMEM)
    smem = pl.BlockSpec(memory_space=pltpu.SMEM)
    hbm = pl.BlockSpec(memory_space=pl.ANY)
    dma = pltpu.SemaphoreType.DMA
    scratch = [
        pltpu.VMEM((3,) + blocks, BF16),
        pltpu.VMEM((tokens, model), BF16),
        pltpu.VMEM((width, model), BF16),
        pltpu.VMEM((heads, 3, views, BLK, HDIM), BF16),
        pltpu.VMEM((heads, 3, views, BLK, HDIM), BF16),
        pltpu.VMEM(blocks, BF16),
        pltpu.VMEM((heads, views, BLK, HDIM), BF16),
        pltpu.VMEM((heads, views, BLK, HDIM), BF16),
        pltpu.VMEM((views, 1, rows), F32),
        pltpu.VMEM((heads, views, BLK, rows), F32),
        pltpu.VMEM((rows, rows), BF16),
        pltpu.VMEM((rows, rows), BF16),
        pltpu.VMEM((heads, views, BLK, HDIM), BF16),
        pltpu.VMEM((heads, views, BLK, HDIM), BF16),
        pltpu.VMEM((tokens, width), BF16),
        pltpu.VMEM((width, tokens), BF16),
        pltpu.VMEM((heads, 3, views, BLK, HDIM), BF16),
        pltpu.VMEM((heads, 3, views, BLK, HDIM), BF16),
        dma((3, 2)),
        dma((2,)),
    ] + [dma((heads, views))] * 8
    if REDUCE:
        scratch += [
            pltpu.VMEM((width, model), BF16),
            pltpu.VMEM((width // 2, model), BF16),
            pltpu.VMEM((width // 2, model), BF16),
            pltpu.VMEM((3, 128, model), BF16),
            pltpu.VMEM((3, 32, model), BF16),
            pltpu.VMEM((4, 32, model // 4), BF16),
            pltpu.VMEM((3, 32, model // 4), BF16),
            pltpu.VMEM((32, model // 4), BF16),
            pltpu.VMEM((32, model // 4), BF16),
            pltpu.VMEM((4, 32, model // 4), BF16),
            dma, dma,
            dma((3,)), dma((3,)), dma((3,)), dma((3,)),
            dma((3,)), dma((3,)), dma, dma, dma((3,)), dma((3,)),
            dma((3,)), dma((3,)), dma((3,)), dma((3,)),
            dma, dma,
        ]
        gw_shape = jax.ShapeDtypeStruct((2, 4, 4, 32, model), BF16)
    else:
        gw_shape = jax.ShapeDtypeStruct((width, model), F32)
    grad_shape = jax.ShapeDtypeStruct(blocks, BF16)
    shapes = (
        jax.ShapeDtypeStruct((tokens, model), BF16),
        grad_shape, grad_shape, grad_shape, gw_shape,
    )
    done = pl.pallas_call(
        functools.partial(kernel, heads, views),
        out_shape=tuple(pltpu.VMEM(s.shape, s.dtype) for s in shapes) if PINNED else shapes,
        in_specs=[hbm] * 5 + [smem] * 2,
        out_specs=[vmem] * 5,
        scratch_shapes=scratch,
        compiler_params=pltpu.CompilerParams(
            collective_id=0, has_side_effects=True, vmem_limit_bytes=51 * 1024 * 1024
        ),
        cost_estimate=pl.CostEstimate(
            flops=9_700_000_000, bytes_accessed=18_000_000, transcendentals=2_100_000
        ),
    )(
        queries.reshape(blocks), keys.reshape(blocks), values.reshape(blocks),
        out_grad.reshape(tokens, model), w_out,
        bucket_of.reshape(views, views), pair_mask.reshape(views, views),
    )
    if PINNED:
        done = [pltpu.with_memory_space_constraint(d, pltpu.VMEM) for d in done]
    layer_out, grad_q, grad_k, grad_v, grad_w = pl.pallas_call(
        write_out,
        out_shape=shapes,
        in_specs=[vmem] * 5,
        out_specs=[hbm] * 5,
        scratch_shapes=[dma((5,))],
        compiler_params=pltpu.CompilerParams(vmem_limit_bytes=1024 * 1024),
    )(*done)
    if REDUCE or TIMING:
        grad_w = grad_w.reshape(width, model).astype(BF16)
    else:
        grad_w = lax.psum(grad_w, ("scene", "view")).astype(BF16)
    shape = queries.shape
    return (
        layer_out.reshape(1, 1, tokens, model),
        grad_q.reshape(shape), grad_k.reshape(shape), grad_v.reshape(shape), grad_w,
    )


def solution(mesh):
    split = P("scene", "view", None, None)
    return jax.shard_map(
        body,
        mesh=mesh,
        in_specs=(split, split, split, split, P(), P("scene", None, None), P("scene", None, None)),
        out_specs=(split, split, split, split, P()),
        check_vma=False,
    )
```
